32 devices in a mesh: grp: 8 (over z, x), fsdp: 4 (over y, core).
Axes of the slice: x: 2, y: 2, z: 4, core: 2. Of those that a mesh axis runs over, the one named last changes fastest.
Arguments:
- text: bfloat16 [4096, 8192], P(('grp', 'fsdp'))
- vision: bfloat16 [512, 8192], P(('grp', 'fsdp'))
- vision_token: int32 [512], P(('grp', 'fsdp')), may hold values from 0 to 4095, as said below
- gain: bfloat16 [8192], P('fsdp'), may hold values from 0.099609375 to 1.8984375
- cotangent: bfloat16 [4096, 8192], P(('grp', 'fsdp')), may hold values from -6 to 6
Outputs:
- vision_grad: bfloat16 [512, 8192], P(('grp', 'fsdp'))
- gain_grad: float32 [8192], P('fsdp')
The draws below stay inside these ranges and needn't reach their ends.
Inputs may be any that keep to these rules, and one draw needn't show every extreme that they name: `vision_token`: device d of the flattened grp+fsdp order holds vision rows d * 16 to (d + 1) * 16 - 1 and token rows d * 128 to (d + 1) * 128 - 1. The rows held in group g go to tokens of group (g + 2) mod 8; a device sends at most 4 rows to any one device, and in every group some device receives exactly 4 rows from every device of its source group. No token receives two rows.
All inputs are finite; a program needn't handle non-finite values.
Results may differ from the reference program's by a relative error of at most 0.001.
Values may be sent and summed in bfloat16 or wider, within the bound.
A program may use at most 64 MiB of HBM per device.

```python
import jax
import jax.numpy as jnp
from jax import lax

D = 8192
TOK_DEV = 128
VIS_DEV = 16
CAP = 4
TOKENS = 4096
N_GRP = 8
N_FSDP = 4


def column_scales(key):
    return jnp.exp(jax.random.uniform(jax.random.fold_in(key, 11), (D,), jnp.float32, -1.15, 1.15))


def scaled_rows(key, count, salt):
    keyed = jax.random.fold_in(key, salt)
    first, second = jax.random.split(keyed, 2)
    base = jax.random.normal(first, (count, D), jnp.float32)
    row_scale = jnp.exp(jax.random.uniform(second, (count, 1), jnp.float32, -1.15, 1.15))
    return base * row_scale * column_scales(key)[None, :]


def draw_text(key, part):
    return scaled_rows(key, TOK_DEV * N_GRP * N_FSDP, 3).astype(jnp.bfloat16)


def draw_vision(key, part):
    return scaled_rows(key, VIS_DEV * N_GRP * N_FSDP, 5).astype(jnp.bfloat16)


def draw_vision_token(key, part):
    keyed = jax.random.fold_in(key, 29)
    key_hot, key_score, key_order, key_place = jax.random.split(keyed, 4)
    sources = N_GRP * N_FSDP
    slots = N_FSDP * CAP
    hot = jax.random.randint(key_hot, (N_GRP,), 0, N_FSDP)
    source_ids = jnp.arange(sources)
    source_group = source_ids // N_FSDP
    source_index = source_ids % N_FSDP
    target_group = (source_group + N_GRP // 4) % N_GRP
    hot_source = hot[target_group]
    slot_ids = jnp.arange(slots)
    score = jax.random.randint(key_score, (sources, slots), 0, 2 ** 20) * slots + slot_ids[None, :]
    score = jnp.where((slot_ids // CAP)[None, :] == hot_source[:, None], score - 2 ** 30, score)
    chosen = jnp.argsort(score, axis=1)[:, :VIS_DEV]
    order_score = jax.random.randint(key_order, (sources, VIS_DEV), 0, 2 ** 20) * VIS_DEV + jnp.arange(VIS_DEV)[None, :]
    chosen = jnp.take_along_axis(chosen, jnp.argsort(order_score, axis=1), axis=1)
    target = chosen // CAP
    within = chosen % CAP
    place_score = jax.random.randint(key_place, (sources, TOK_DEV), 0, 2 ** 20) * TOK_DEV + jnp.arange(TOK_DEV)[None, :]
    places = jnp.argsort(place_score, axis=1)
    target_device = target_group[:, None] * N_FSDP + target
    rank = source_index[:, None] * CAP + within
    position = places[target_device, rank]
    return (target_device * TOK_DEV + position).reshape(-1).astype(jnp.int32)


def strengthened(array, rng, source, target, shards_of, factor):
    def block_of(dim):
        return (jnp.arange(array.shape[dim]) // (array.shape[dim] // shards_of)).reshape((-1,) + (1,) * (array.ndim - 1 - dim))

    one_side = jax.random.permutation(rng, shards_of)[block_of(target)]
    far = (block_of(target) + shards_of // 2) % shards_of
    return jnp.where((block_of(source) == one_side) | (block_of(source) == far), factor * array, array)


def block_scale(own_key, extent, cuts, least, high):
    loudness = 1.0
    for axis_at, parts in cuts:
        draws = jax.random.uniform(jax.random.fold_in(jax.random.fold_in(own_key, 6), axis_at), (parts,), jnp.float32, least / len(cuts), high / len(cuts))
        loudness = loudness * jnp.repeat(jnp.exp(draws), extent[axis_at] // parts).reshape((-1,) + (1,) * (len(extent) - 1 - axis_at))
    return loudness


def gaussian_with(stream_key, dims, width, bound, pieces, heavy, dtype=jnp.bfloat16):
    values = width * jax.random.normal(stream_key, dims, jnp.float32)
    if pieces:
        values = values * block_scale(stream_key, dims, pieces, -0.22, 0.18)
    return jnp.clip(strengthened(values, jax.random.fold_in(stream_key, 3), *heavy), -bound, bound).astype(dtype)


def setup_inputs(seed: int = 0) -> dict:
    splits = jax.random.split(jax.random.key(seed), 6)
    text = draw_text(jax.random.fold_in(splits[5], 71), 0)
    vision = draw_vision(jax.random.fold_in(splits[5], 71), 0)
    vision_token = draw_vision_token(jax.random.fold_in(splits[5], 71), 0)
    gain = jnp.clip(1.0 + 0.18 * jax.random.normal(splits[3], (D,), jnp.float32), 0.099609375, 1.8984375).astype(jnp.bfloat16)
    cotangent = gaussian_with(splits[4], (TOKENS, D), 1.0, 6.0, ((0, 32),), (0, 1, 32, 2.75))
    return {"text": text, "vision": vision, "vision_token": vision_token, "gain": gain, "cotangent": cotangent}


def reference(text, vision, vision_token, gain, cotangent):
    assembled = text.at[vision_token].set(vision)
    scale_row = gain.astype(jnp.float32)
    blocks = assembled.reshape(-1, TOK_DEV, D)
    cot_blocks = cotangent.reshape(-1, TOK_DEV, D)

    def advance(total, pair):
        rows, grads = pair
        values = rows.astype(jnp.float32)
        upper = grads.astype(jnp.float32)
        inv = lax.rsqrt(lax.optimization_barrier(jnp.mean(values * values, axis=-1, keepdims=True)) + 1e-06)
        scaled = upper * scale_row
        inner = lax.optimization_barrier(jnp.mean(values * scaled, axis=-1, keepdims=True))
        token_grad = inv * scaled - values * inv * inv * inv * inner
        total = total + lax.optimization_barrier(jnp.sum(upper * values * inv, axis=0))
        return (total, token_grad.astype(jnp.bfloat16))
    total, token_grad = lax.scan(advance, jnp.zeros((D,), jnp.float32), (blocks, cot_blocks))
    token_grad = token_grad.reshape(-1, D)
    return (token_grad[vision_token], total)
```

```python
import functools

import jax
import jax.numpy as jnp
from jax import lax
from jax.experimental import pallas as pl
from jax.experimental.pallas import tpu as pltpu
from jax.sharding import PartitionSpec as P

MESH = pl.DeviceIdType.MESH
F32 = jnp.float32
LANES = 128
PIECES = 4


def one_where(condition):
    return jnp.where(condition, 1.0, 0.0).astype(F32)


def iota(shape, dim):
    return lax.broadcasted_iota(jnp.int32, shape, dim).astype(F32)


def as_column(row):
    n = row.shape[1]
    diagonal = iota((n, n), 0) == iota((n, n), 1)
    return jnp.sum(jnp.where(diagonal, jnp.broadcast_to(row, (n, n)), 0.0), axis=1, keepdims=True)


def fold(value):
    total = value[0:8]
    for at in range(8, value.shape[0], 8):
        total = total + value[at : at + 8]
    return total


def kernel(
    n_grp, n_fsdp, hop, capacity,
    token_ref, gain_ref, vision_ref, text_hbm, cot_hbm,
    grad_ref, share_ref,
    text, cot, token_out, tokens, gains, rows_out, rows_in, own, terms, first_out, first_in, second,
    load_sem, token_send, token_recv, gain_send, gain_recv, rows_send, rows_recv,
    first_send, first_recv, second_send, second_recv,
):
    g, f = lax.axis_index("grp"), lax.axis_index("fsdp")
    tok_dev, width = text.shape
    vis_dev = vision_ref.shape[0]
    share = width // n_fsdp
    piece = share // PIECES
    block = capacity * n_fsdp
    ahead, behind = lax.rem(g + hop, n_grp), lax.rem(g + n_grp - hop, n_grp)

    load_cot = pltpu.make_async_copy(cot_hbm, cot, load_sem.at[0])
    load_text = pltpu.make_async_copy(text_hbm, text, load_sem.at[1])
    load_text.start()
    load_cot.start()

    barrier = pltpu.get_barrier_semaphore()
    for s in range(n_fsdp):
        pl.semaphore_signal(barrier, inc=1, device_id=(ahead, s), device_id_type=MESH)
        pl.semaphore_signal(barrier, inc=1, device_id=(behind, s), device_id_type=MESH)
    for d in range(1, n_fsdp):
        pl.semaphore_signal(barrier, inc=1, device_id=(g, lax.rem(f + d, n_fsdp)), device_id_type=MESH)

    def greet(d, carry):
        pl.semaphore_signal(barrier, inc=1, device_id=(lax.rem(g + d, n_grp), f), device_id_type=MESH)
        return carry

    lax.fori_loop(1, n_grp, greet, 0)
    token_out[...] = jnp.zeros_like(token_out)
    token_out[:, 0:vis_dev] = token_ref[...]
    gains[f] = gain_ref[...].astype(F32)
    pl.semaphore_wait(barrier, 3 * n_fsdp + n_grp - 2)

    token_copies = []
    for s in range(n_fsdp):
        copy = pltpu.make_async_remote_copy(
            token_out, tokens.at[f], token_send.at[s], token_recv.at[f],
            device_id=(ahead, s), device_id_type=MESH,
        )
        copy.start()
        token_copies.append(copy)
    gain_copies = []
    for d in range(1, n_fsdp):
        copy = pltpu.make_async_remote_copy(
            gains.at[f], gains.at[f], gain_send.at[d - 1], gain_recv.at[d - 1],
            device_id=(g, lax.rem(f + d, n_fsdp)), device_id_type=MESH,
        )
        copy.start()
        gain_copies.append(copy)

    load_text.wait()

    def squares(c, total):
        value = text[:, pl.ds(pl.multiple_of(c * LANES, LANES), LANES)].astype(F32)
        return total + value * value

    total = lax.fori_loop(0, width // LANES, squares, jnp.zeros((tok_dev, LANES), F32), unroll=4)
    inv = lax.rsqrt(jnp.sum(total, axis=1, keepdims=True) / width + 1e-06)
    total = jnp.zeros((vis_dev, LANES), F32)
    for c in range(0, width, LANES):
        value = vision_ref[:, c : c + LANES].astype(F32)
        total = total + value * value
    inv_vision = lax.rsqrt(jnp.sum(total, axis=1, keepdims=True) / width + 1e-06)

    mine = token_ref[...].astype(F32)
    mine_column = as_column(mine)
    start = (ahead * (n_fsdp * tok_dev)).astype(F32)
    target_row, target_column = jnp.zeros_like(mine), jnp.zeros_like(mine_column)
    for t in range(1, n_fsdp):
        target_row += one_where(mine >= start + float(t * tok_dev))
        target_column += one_where(mine_column >= start + float(t * tok_dev))
    square = (vis_dev, vis_dev)
    same = one_where((target_row == target_column) & (iota(square, 1) < iota(square, 0)))
    rank_column = jnp.sum(same, axis=1, keepdims=True)
    wide = (vis_dev, n_fsdp * block)
    places = []
    for q in range(n_fsdp):
        slot = target_column * block + (q * capacity) + rank_column
        places.append(one_where(iota(wide, 1) == slot).astype(jnp.bfloat16))

    base = ((g * n_fsdp + f) * tok_dev).astype(F32)
    marks = jnp.zeros((tok_dev, vis_dev), F32)
    asked = []
    for s in range(n_fsdp):
        pltpu.make_async_remote_copy(
            token_out, tokens.at[s], token_send.at[s], token_recv.at[s],
            device_id=(behind, s), device_id_type=MESH,
        ).wait_recv()
        row = tokens[s][:, 0:vis_dev].astype(F32) - base
        column = as_column(row)
        marks += one_where(iota((tok_dev, vis_dev), 0) == row)
        here_row = (row >= 0.0) & (row < float(tok_dev))
        here_column = one_where((column >= 0.0) & (column < float(tok_dev)))
        rank_row = jnp.sum(
            jnp.where(iota(square, 0) < iota(square, 1), jnp.broadcast_to(here_column, square), 0.0),
            axis=0, keepdims=True,
        )
        rank_row = jnp.where(here_row, rank_row, -1.0)
        hit = one_where(iota((vis_dev, tok_dev), 1) == column)
        line = lax.broadcasted_iota(jnp.int32, (block, vis_dev), 0)
        pick = one_where(lax.rem(line, capacity).astype(F32) == rank_row)
        asked.append(
            jnp.dot(pick.astype(jnp.bfloat16), hit.astype(jnp.bfloat16), preferred_element_type=F32)
        )
    asked = jnp.concatenate(asked, axis=0)
    line = lax.rem(lax.broadcasted_iota(jnp.int32, asked.shape, 0), block)
    picks = [
        jnp.where((line >= q * capacity) & (line < (q + 1) * capacity), asked, 0.0).astype(jnp.bfloat16)
        for q in range(n_fsdp)
    ]

    load_cot.wait()
    row_copies = []
    for k in range(PIECES):
        picked = jnp.zeros((n_fsdp * block, piece), F32)
        for q in range(n_fsdp):
            at = q * share + k * piece
            picked += jnp.dot(picks[q], cot[:, at : at + piece], preferred_element_type=F32)
        rows_out[:, :, k * piece : (k + 1) * piece] = picked.astype(jnp.bfloat16).reshape(n_fsdp, block, piece)
        for s in range(n_fsdp):
            copy = pltpu.make_async_remote_copy(
                rows_out.at[s, :, k * piece : (k + 1) * piece],
                rows_in.at[f, :, k * piece : (k + 1) * piece],
                rows_send.at[k, s], rows_recv.at[k, f],
                device_id=(behind, s), device_id_type=MESH,
            )
            copy.start()
            row_copies.append(copy)

    weight = jnp.broadcast_to(inv * (1.0 - jnp.sum(marks, axis=1, keepdims=True)), (tok_dev, LANES))

    def text_terms(c, carry):
        at = pl.ds(pl.multiple_of(c * LANES, LANES), LANES)
        terms[:, at] = fold(cot[:, at].astype(F32) * text[:, at].astype(F32) * weight)
        return carry

    lax.fori_loop(0, width // LANES, text_terms, 0, unroll=2)

    for copy in gain_copies:
        copy.wait_send()
    for d in range(1, n_fsdp):
        source = lax.rem(f + n_fsdp - d, n_fsdp)
        pltpu.make_async_remote_copy(
            gains.at[f], gains.at[source], gain_send.at[d - 1], gain_recv.at[d - 1],
            device_id=(g, source), device_id_type=MESH,
        ).wait_recv()

    inner = jnp.zeros((vis_dev, 1), F32)
    for k in range(PIECES):
        cut = slice(k * piece, (k + 1) * piece)
        for s in range(n_fsdp):
            pltpu.make_async_remote_copy(
                rows_out.at[s, :, cut], rows_in.at[s, :, cut],
                rows_send.at[k, s], rows_recv.at[k, s],
                device_id=(ahead, s), device_id_type=MESH,
            ).wait_recv()
        arrived = rows_in[:, :, cut].reshape(n_fsdp * block, piece)
        for q in range(n_fsdp):
            at = q * share + k * piece
            upper = jnp.dot(places[q], arrived, preferred_element_type=F32)
            value = vision_ref[:, at : at + piece].astype(F32)
            product = upper * value
            terms[:, at : at + piece] += fold(product * inv_vision)
            inner += jnp.sum(product * gains[q, :, cut], axis=1, keepdims=True)
            own[:, at : at + piece] = upper

    for q in range(n_fsdp):
        first_out[q] = jnp.sum(terms[:, q * share : (q + 1) * share], axis=0, keepdims=True)
    first_copies = []
    for d in range(1, n_fsdp):
        peer = lax.rem(f + d, n_fsdp)
        copy = pltpu.make_async_remote_copy(
            first_out.at[peer], first_in.at[d - 1], first_send.at[d - 1], first_recv.at[d - 1],
            device_id=(g, peer), device_id_type=MESH,
        )
        copy.start()
        first_copies.append(copy)

    factor = inv_vision * inv_vision * inv_vision * (inner / width)
    for q in range(n_fsdp):
        for k in range(PIECES):
            at = q * share + k * piece
            scaled = own[:, at : at + piece] * gains[q, :, k * piece : (k + 1) * piece]
            value = vision_ref[:, at : at + piece].astype(F32)
            grad_ref[:, at : at + piece] = (inv_vision * scaled - value * factor).astype(jnp.bfloat16)

    part = first_out[f]
    for d in range(1, n_fsdp):
        first_copies[d - 1].wait_recv()
        part = part + first_in[d - 1]
    second[g] = part

    def send(d, carry):
        peer = lax.rem(g + d, n_grp)
        pltpu.make_async_remote_copy(
            second.at[g], second.at[g], second_send.at[peer], second_recv.at[g],
            device_id=(peer, f), device_id_type=MESH,
        ).start()
        return carry

    def arrive(d, carry):
        peer = lax.rem(g + d, n_grp)
        copy = pltpu.make_async_remote_copy(
            second.at[peer], second.at[peer], second_send.at[peer], second_recv.at[peer],
            device_id=(peer, f), device_id_type=MESH,
        )
        copy.wait_recv()
        copy.wait_send()
        return carry

    lax.fori_loop(1, n_grp, send, 0)
    for copy in token_copies + row_copies + first_copies:
        copy.wait_send()
    lax.fori_loop(1, n_grp, arrive, 0)
    whole = second[0]
    for at in range(1, n_grp):
        whole = whole + second[at]
    share_ref[...] = whole


def shards(n_grp, n_fsdp, text, vision, vision_token, gain, cotangent):
    hop = n_grp // 4
    tok_dev, width = text.shape
    vis_dev = vision.shape[0]
    capacity = vis_dev // 4
    share = width // n_fsdp
    block = capacity * n_fsdp
    bf16 = jnp.bfloat16
    vmem, dma = pltpu.VMEM, pltpu.SemaphoreType.DMA
    inside = pl.BlockSpec(memory_space=pltpu.VMEM)
    outside = pl.BlockSpec(memory_space=pl.ANY)
    vision_grad, gain_grad = pl.pallas_call(
        functools.partial(kernel, n_grp, n_fsdp, hop, capacity),
        out_shape=(
            jax.ShapeDtypeStruct((vis_dev, width), bf16),
            jax.ShapeDtypeStruct((1, share), F32),
        ),
        in_specs=[inside, inside, inside, outside, outside],
        out_specs=(inside, inside),
        scratch_shapes=[
            vmem((tok_dev, width), bf16),
            vmem((tok_dev, width), bf16),
            vmem((1, LANES), jnp.int32),
            vmem((n_fsdp, 1, LANES), jnp.int32),
            vmem((n_fsdp, 1, share), F32),
            vmem((n_fsdp, block, share), bf16),
            vmem((n_fsdp, block, share), bf16),
            vmem((vis_dev, width), F32),
            vmem((8, width), F32),
            vmem((n_fsdp, 1, share), F32),
            vmem((n_fsdp - 1, 1, share), F32),
            vmem((n_grp, 1, share), F32),
            dma((2,)),
            dma((n_fsdp,)),
            dma((n_fsdp,)),
            dma((n_fsdp - 1,)),
            dma((n_fsdp - 1,)),
            dma((PIECES, n_fsdp)),
            dma((PIECES, n_fsdp)),
            dma((n_fsdp - 1,)),
            dma((n_fsdp - 1,)),
            dma((n_grp,)),
            dma((n_grp,)),
        ],
        compiler_params=pltpu.CompilerParams(
            collective_id=0, has_side_effects=True, vmem_limit_bytes=32 * 1024 * 1024
        ),
    )(vision_token.reshape(1, vis_dev), gain.reshape(1, share), vision, text, cotangent)
    return (vision_grad, gain_grad.reshape(share))


def solution(mesh):
    return jax.shard_map(
        functools.partial(shards, mesh.shape["grp"], mesh.shape["fsdp"]),
        mesh=mesh,
        in_specs=(
            P(("grp", "fsdp"), None),
            P(("grp", "fsdp"), None),
            P(("grp", "fsdp")),
            P("fsdp"),
            P(("grp", "fsdp"), None),
        ),
        out_specs=(P(("grp", "fsdp"), None), P("fsdp")),
        check_vma=False,
    )
```

```python
import functools

import jax
import jax.numpy as jnp
from jax import lax
from jax.experimental import pallas as pl
from jax.experimental.pallas import tpu as pltpu
from jax.sharding import PartitionSpec as P

MESH = pl.DeviceIdType.MESH
F32 = jnp.float32
LANES = 128
PIECES = 4


def one_where(condition):
    return jnp.where(condition, 1.0, 0.0).astype(F32)


def iota(shape, dim):
    return lax.broadcasted_iota(jnp.int32, shape, dim).astype(F32)


def as_column(row):
    n = row.shape[1]
    diagonal = iota((n, n), 0) == iota((n, n), 1)
    return jnp.sum(jnp.where(diagonal, jnp.broadcast_to(row, (n, n)), 0.0), axis=1, keepdims=True)


def fold(value):
    total = value[0:8]
    for at in range(8, value.shape[0], 8):
        total = total + value[at : at + 8]
    return total


def kernel(
    n_grp, n_fsdp, hop, capacity,
    token_hbm, gain_hbm, vision_hbm, text_hbm, cot_hbm,
    grad_ref, share_ref,
    text, cot, vision_ref, token_ref, slots_out, slots_in, gains, rows_out, rows_in, own, terms,
    first_out, first_in, second,
    load_sem, slot_send, slot_recv, gain_send, gain_recv, rows_send, rows_recv,
    first_send, first_recv, second_send, second_recv,
):
    g, f = lax.axis_index("grp"), lax.axis_index("fsdp")
    tok_dev, width = text.shape
    vis_dev = vision_ref.shape[0]
    share = width // n_fsdp
    piece = share // PIECES
    block = capacity * n_fsdp
    lines = slots_out.shape[1]
    ahead, behind = lax.rem(g + hop, n_grp), lax.rem(g + n_grp - hop, n_grp)

    load_token = pltpu.make_async_copy(token_hbm, token_ref, load_sem.at[0])
    load_gain = pltpu.make_async_copy(gain_hbm, gains.at[f], load_sem.at[1])
    load_cot = pltpu.make_async_copy(cot_hbm, cot, load_sem.at[2])
    load_vision = pltpu.make_async_copy(vision_hbm, vision_ref, load_sem.at[3])
    load_text = pltpu.make_async_copy(text_hbm, text, load_sem.at[4])
    load_token.start()

    barrier = pltpu.get_barrier_semaphore()
    for s in range(n_fsdp):
        pl.semaphore_signal(barrier, inc=1, device_id=(ahead, s), device_id_type=MESH)
        pl.semaphore_signal(barrier, inc=1, device_id=(behind, s), device_id_type=MESH)
    for d in range(1, n_fsdp):
        pl.semaphore_signal(barrier, inc=1, device_id=(g, lax.rem(f + d, n_fsdp)), device_id_type=MESH)

    def greet(d, carry):
        pl.semaphore_signal(barrier, inc=1, device_id=(lax.rem(g + d, n_grp), f), device_id_type=MESH)
        return carry

    lax.fori_loop(1, n_grp, greet, 0)
    load_gain.start()
    load_cot.start()
    load_vision.start()
    load_text.start()

    load_token.wait()
    mine = token_ref[...].astype(F32) - (ahead * (n_fsdp * tok_dev)).astype(F32)
    mine_column = as_column(mine)
    target_row, target_column = jnp.zeros_like(mine), jnp.zeros_like(mine_column)
    for t in range(1, n_fsdp):
        target_row += one_where(mine >= float(t * tok_dev))
        target_column += one_where(mine_column >= float(t * tok_dev))
    square = (vis_dev, vis_dev)
    same = target_row == target_column
    rank_column = jnp.sum(
        one_where(same & (iota(square, 1) < iota(square, 0))), axis=1, keepdims=True
    )
    rank_row = jnp.sum(
        one_where(same & (iota(square, 0) < iota(square, 1))), axis=0, keepdims=True
    )
    local = mine - target_row * float(tok_dev)
    line = lax.rem(lax.broadcasted_iota(jnp.int32, (lines, vis_dev), 0), capacity).astype(F32)
    for t in range(n_fsdp):
        chosen = (line == rank_row) & (target_row == float(t))
        number = jnp.sum(jnp.where(chosen, local + 1.0, 0.0), axis=1, keepdims=True) - 1.0
        slots_out[t] = jnp.broadcast_to(number, (lines, LANES))
    pl.semaphore_wait(barrier, 3 * n_fsdp + n_grp - 2)

    slot_copies = []
    for s in range(n_fsdp):
        copy = pltpu.make_async_remote_copy(
            slots_out.at[s], slots_in.at[f], slot_send.at[s], slot_recv.at[f],
            device_id=(ahead, s), device_id_type=MESH,
        )
        copy.start()
        slot_copies.append(copy)
    load_gain.wait()
    gain_copies = []
    for d in range(1, n_fsdp):
        copy = pltpu.make_async_remote_copy(
            gains.at[f], gains.at[f], gain_send.at[d - 1], gain_recv.at[d - 1],
            device_id=(g, lax.rem(f + d, n_fsdp)), device_id_type=MESH,
        )
        copy.start()
        gain_copies.append(copy)

    wide = (vis_dev, n_fsdp * block)
    places = []
    for q in range(n_fsdp):
        slot = target_column * block + (q * capacity) + rank_column
        places.append(one_where(iota(wide, 1) == slot).astype(jnp.bfloat16))
    load_vision.wait()
    total = jnp.zeros((vis_dev, LANES), F32)
    for c in range(0, width, LANES):
        value = vision_ref[:, c : c + LANES].astype(F32)
        total = total + value * value
    inv_vision = lax.rsqrt(jnp.sum(total, axis=1, keepdims=True) / width + 1e-06)
    load_cot.wait()

    asked = []
    for s in range(n_fsdp):
        pltpu.make_async_remote_copy(
            slots_out.at[s], slots_in.at[s], slot_send.at[s], slot_recv.at[s],
            device_id=(behind, s), device_id_type=MESH,
        ).wait_recv()
        number = slots_in[s][:, 0:tok_dev] if tok_dev <= LANES else pltpu.repeat(slots_in[s], tok_dev // LANES, 1)
        asked += [one_where(iota((lines, tok_dev), 1) == number)] * (block // lines)
    asked = jnp.concatenate(asked, axis=0)
    line = lax.rem(lax.broadcasted_iota(jnp.int32, asked.shape, 0), block)
    picks = [
        jnp.where((line >= q * capacity) & (line < (q + 1) * capacity), asked, 0.0).astype(jnp.bfloat16)
        for q in range(n_fsdp)
    ]
    row_copies = []
    for k in range(PIECES):
        picked = jnp.zeros((n_fsdp * block, piece), F32)
        for q in range(n_fsdp):
            at = q * share + k * piece
            picked += jnp.dot(picks[q], cot[:, at : at + piece], preferred_element_type=F32)
        rows_out[:, :, k * piece : (k + 1) * piece] = picked.astype(jnp.bfloat16).reshape(n_fsdp, block, piece)
        for s in range(n_fsdp):
            copy = pltpu.make_async_remote_copy(
                rows_out.at[s, :, k * piece : (k + 1) * piece],
                rows_in.at[f, :, k * piece : (k + 1) * piece],
                rows_send.at[k, s], rows_recv.at[k, f],
                device_id=(behind, s), device_id_type=MESH,
            )
            copy.start()
            row_copies.append(copy)

    load_text.wait()

    def squares(c, total):
        value = text[:, pl.ds(pl.multiple_of(c * LANES, LANES), LANES)].astype(F32)
        return total + value * value

    total = lax.fori_loop(0, width // LANES, squares, jnp.zeros((tok_dev, LANES), F32), unroll=4)
    inv = lax.rsqrt(jnp.sum(total, axis=1, keepdims=True) / width + 1e-06)
    marks = as_column(jnp.sum(jnp.where(line < capacity, asked, 0.0), axis=0, keepdims=True))
    weight = jnp.broadcast_to(inv * (1.0 - marks), (tok_dev, LANES))

    def text_terms(c, carry):
        at = pl.ds(pl.multiple_of(c * LANES, LANES), LANES)
        terms[:, at] = fold(cot[:, at].astype(F32) * text[:, at].astype(F32) * weight)
        return carry

    lax.fori_loop(0, width // LANES, text_terms, 0, unroll=2)

    for copy in gain_copies:
        copy.wait_send()
    for d in range(1, n_fsdp):
        source = lax.rem(f + n_fsdp - d, n_fsdp)
        pltpu.make_async_remote_copy(
            gains.at[f], gains.at[source], gain_send.at[d - 1], gain_recv.at[d - 1],
            device_id=(g, source), device_id_type=MESH,
        ).wait_recv()

    gain_rows = []
    for q in range(n_fsdp):
        tiles = gains[q].astype(F32)
        flat = jnp.concatenate([tiles[c : c + 1] for c in range(tiles.shape[0])], axis=1)
        gain_rows.append([flat[:, k * piece : (k + 1) * piece] for k in range(PIECES)])

    inner = jnp.zeros((vis_dev, LANES), F32)
    for k in range(PIECES):
        cut = slice(k * piece, (k + 1) * piece)
        for s in range(n_fsdp):
            pltpu.make_async_remote_copy(
                rows_out.at[s, :, cut], rows_in.at[s, :, cut],
                rows_send.at[k, s], rows_recv.at[k, s],
                device_id=(ahead, s), device_id_type=MESH,
            ).wait_recv()
        arrived = rows_in[:, :, cut].reshape(n_fsdp * block, piece)
        for q in range(n_fsdp):
            at = q * share + k * piece
            upper = jnp.dot(places[q], arrived, preferred_element_type=F32)
            value = vision_ref[:, at : at + piece].astype(F32)
            product = upper * value
            terms[:, at : at + piece] += fold(product * inv_vision)
            product = product * gain_rows[q][k]
            for c in range(0, piece, LANES):
                inner += product[:, c : c + LANES]
            own[:, at : at + piece] = upper

    for q in range(n_fsdp):
        first_out[q] = jnp.sum(terms[:, q * share : (q + 1) * share], axis=0, keepdims=True)
    first_copies = []
    for d in range(1, n_fsdp):
        peer = lax.rem(f + d, n_fsdp)
        copy = pltpu.make_async_remote_copy(
            first_out.at[peer], first_in.at[d - 1], first_send.at[d - 1], first_recv.at[d - 1],
            device_id=(g, peer), device_id_type=MESH,
        )
        copy.start()
        first_copies.append(copy)

    inner = jnp.sum(inner, axis=1, keepdims=True) / width
    factor = inv_vision * inv_vision * inv_vision * inner
    for q in range(n_fsdp):
        for k in range(PIECES):
            at = q * share + k * piece
            scaled = own[:, at : at + piece] * gain_rows[q][k]
            value = vision_ref[:, at : at + piece].astype(F32)
            grad_ref[:, at : at + piece] = (inv_vision * scaled - value * factor).astype(jnp.bfloat16)

    part = first_out[f]
    for d in range(1, n_fsdp):
        first_copies[d - 1].wait_recv()
        part = part + first_in[d - 1]
    second[g] = part

    def send(d, carry):
        peer = lax.rem(g + d, n_grp)
        pltpu.make_async_remote_copy(
            second.at[g], second.at[g], second_send.at[peer], second_recv.at[g],
            device_id=(peer, f), device_id_type=MESH,
        ).start()
        return carry

    def arrive(d, carry):
        peer = lax.rem(g + d, n_grp)
        copy = pltpu.make_async_remote_copy(
            second.at[peer], second.at[peer], second_send.at[peer], second_recv.at[peer],
            device_id=(peer, f), device_id_type=MESH,
        )
        copy.wait_recv()
        copy.wait_send()
        return carry

    lax.fori_loop(1, n_grp, send, 0)
    for copy in slot_copies + row_copies + first_copies:
        copy.wait_send()
    lax.fori_loop(1, n_grp, arrive, 0)
    whole = second[0]
    for at in range(1, n_grp):
        whole = whole + second[at]
    share_ref[...] = whole


def shards(n_grp, n_fsdp, text, vision, vision_token, gain, cotangent):
    hop = n_grp // 4
    tok_dev, width = text.shape
    vis_dev = vision.shape[0]
    capacity = vis_dev // 4
    share = width // n_fsdp
    block = capacity * n_fsdp
    bf16 = jnp.bfloat16
    vmem, dma = pltpu.VMEM, pltpu.SemaphoreType.DMA
    inside = pl.BlockSpec(memory_space=pltpu.VMEM)
    outside = pl.BlockSpec(memory_space=pltpu.HBM)
    vision_grad, gain_grad = pl.pallas_call(
        functools.partial(kernel, n_grp, n_fsdp, hop, capacity),
        out_shape=(
            jax.ShapeDtypeStruct((vis_dev, width), bf16),
            jax.ShapeDtypeStruct((1, share), F32),
        ),
        in_specs=[outside] * 5,
        out_specs=(inside, inside),
        scratch_shapes=[
            vmem((tok_dev, width), bf16),
            vmem((tok_dev, width), bf16),
            vmem((vis_dev, width), bf16),
            vmem((1, vis_dev), jnp.int32),
            vmem((n_fsdp, 2 * capacity, LANES), F32),
            vmem((n_fsdp, 2 * capacity, LANES), F32),
            vmem((n_fsdp, share // LANES, LANES), bf16),
            vmem((n_fsdp, block, share), bf16),
            vmem((n_fsdp, block, share), bf16),
            vmem((vis_dev, width), F32),
            vmem((8, width), F32),
            vmem((n_fsdp, 1, share), F32),
            vmem((n_fsdp - 1, 1, share), F32),
            vmem((n_grp, 1, share), F32),
            dma((5,)),
            dma((n_fsdp,)),
            dma((n_fsdp,)),
            dma((n_fsdp - 1,)),
            dma((n_fsdp - 1,)),
            dma((PIECES, n_fsdp)),
            dma((PIECES, n_fsdp)),
            dma((n_fsdp - 1,)),
            dma((n_fsdp - 1,)),
            dma((n_grp,)),
            dma((n_grp,)),
        ],
        compiler_params=pltpu.CompilerParams(
            collective_id=0, has_side_effects=True, vmem_limit_bytes=56 * 1024 * 1024
        ),
    )(vision_token.reshape(1, vis_dev), gain.reshape(share // LANES, LANES), vision, text, cotangent)
    return (vision_grad, gain_grad.reshape(share))


def solution(mesh):
    return jax.shard_map(
        functools.partial(shards, mesh.shape["grp"], mesh.shape["fsdp"]),
        mesh=mesh,
        in_specs=(
            P(("grp", "fsdp"), None),
            P(("grp", "fsdp"), None),
            P(("grp", "fsdp")),
            P("fsdp"),
            P(("grp", "fsdp"), None),
        ),
        out_specs=(P(("grp", "fsdp"), None), P("fsdp")),
        check_vma=False,
    )
```

```python
import functools

import jax
import jax.numpy as jnp
from jax import lax
from jax.experimental import pallas as pl
from jax.experimental.pallas import tpu as pltpu
from jax.sharding import PartitionSpec as P

MESH = pl.DeviceIdType.MESH
F32 = jnp.float32
LANES = 128
PIECES = 4


def one_where(condition):
    return jnp.where(condition, 1.0, 0.0).astype(F32)


def iota(shape, dim):
    return lax.broadcasted_iota(jnp.int32, shape, dim).astype(F32)


def as_column(row):
    n = row.shape[1]
    diagonal = iota((n, n), 0) == iota((n, n), 1)
    return jnp.sum(jnp.where(diagonal, jnp.broadcast_to(row, (n, n)), 0.0), axis=1, keepdims=True)


def fold(value):
    total = value[0:8]
    for at in range(8, value.shape[0], 8):
        total = total + value[at : at + 8]
    return total


def kernel(
    n_grp, n_fsdp, hop, capacity,
    token_hbm, gain_hbm, vision_hbm, text_hbm, cot_hbm,
    grad_ref, share_ref,
    text, cot, vision_ref, token_ref, slots_out, slots_in, gains, rows_out, rows_in, own, terms,
    first_out, first_in, second,
    load_sem, slot_send, slot_recv, gain_send, gain_recv, rows_send, rows_recv,
    first_send, first_recv, second_send, second_recv,
):
    g, f = lax.axis_index("grp"), lax.axis_index("fsdp")
    tok_dev, width = text.shape
    vis_dev = vision_ref.shape[0]
    share = width // n_fsdp
    piece = share // PIECES
    block = capacity * n_fsdp
    lines = slots_out.shape[1]
    ahead, behind = lax.rem(g + hop, n_grp), lax.rem(g + n_grp - hop, n_grp)

    load_token = pltpu.make_async_copy(token_hbm, token_ref, load_sem.at[0])
    load_gain = pltpu.make_async_copy(gain_hbm, gains.at[f], load_sem.at[1])
    load_cot = pltpu.make_async_copy(cot_hbm, cot, load_sem.at[2])
    load_vision = pltpu.make_async_copy(vision_hbm, vision_ref, load_sem.at[3])
    load_text = pltpu.make_async_copy(text_hbm, text, load_sem.at[4])
    load_token.start()

    barrier = pltpu.get_barrier_semaphore()
    for s in range(n_fsdp):
        pl.semaphore_signal(barrier, inc=1, device_id=(ahead, s), device_id_type=MESH)
        pl.semaphore_signal(barrier, inc=1, device_id=(behind, s), device_id_type=MESH)
    for d in range(1, n_fsdp):
        pl.semaphore_signal(barrier, inc=1, device_id=(g, lax.rem(f + d, n_fsdp)), device_id_type=MESH)

    def greet(d, carry):
        pl.semaphore_signal(barrier, inc=1, device_id=(lax.rem(g + d, n_grp), f), device_id_type=MESH)
        return carry

    lax.fori_loop(1, n_grp, greet, 0)
    load_gain.start()
    load_cot.start()
    load_vision.start()
    load_text.start()

    load_token.wait()
    mine = token_ref[...].astype(F32) - (ahead * (n_fsdp * tok_dev)).astype(F32)
    mine_column = as_column(mine)
    target_row, target_column = jnp.zeros_like(mine), jnp.zeros_like(mine_column)
    for t in range(1, n_fsdp):
        target_row += one_where(mine >= float(t * tok_dev))
        target_column += one_where(mine_column >= float(t * tok_dev))
    square = (vis_dev, vis_dev)
    same = target_row == target_column
    rank_column = jnp.sum(
        one_where(same & (iota(square, 1) < iota(square, 0))), axis=1, keepdims=True
    )
    rank_row = jnp.sum(
        one_where(same & (iota(square, 0) < iota(square, 1))), axis=0, keepdims=True
    )
    local = mine - target_row * float(tok_dev)
    line = lax.rem(lax.broadcasted_iota(jnp.int32, (lines, vis_dev), 0), capacity).astype(F32)
    for t in range(n_fsdp):
        chosen = (line == rank_row) & (target_row == float(t))
        number = jnp.sum(jnp.where(chosen, local + 1.0, 0.0), axis=1, keepdims=True) - 1.0
        slots_out[t] = jnp.broadcast_to(number, (lines, LANES))
    pl.semaphore_wait(barrier, 3 * n_fsdp + n_grp - 2)

    slot_copies = []
    for s in range(n_fsdp):
        copy = pltpu.make_async_remote_copy(
            slots_out.at[s], slots_in.at[f], slot_send.at[s], slot_recv.at[f],
            device_id=(ahead, s), device_id_type=MESH,
        )
        copy.start()
        slot_copies.append(copy)
    load_gain.wait()
    gain_copies = []
    for d in range(1, n_fsdp):
        copy = pltpu.make_async_remote_copy(
            gains.at[f], gains.at[f], gain_send.at[d - 1], gain_recv.at[d - 1],
            device_id=(g, lax.rem(f + d, n_fsdp)), device_id_type=MESH,
        )
        copy.start()
        gain_copies.append(copy)

    wide = (vis_dev, n_fsdp * block)
    places = []
    for q in range(n_fsdp):
        slot = target_column * block + (q * capacity) + rank_column
        places.append(one_where(iota(wide, 1) == slot).astype(jnp.bfloat16))
    load_vision.wait()
    total = jnp.zeros((vis_dev, LANES), F32)
    for c in range(0, width, LANES):
        value = vision_ref[:, c : c + LANES].astype(F32)
        total = total + value * value
    inv_vision = lax.rsqrt(jnp.sum(total, axis=1, keepdims=True) / width + 1e-06)
    load_cot.wait()

    asked = []
    for s in range(n_fsdp):
        pltpu.make_async_remote_copy(
            slots_out.at[s], slots_in.at[s], slot_send.at[s], slot_recv.at[s],
            device_id=(behind, s), device_id_type=MESH,
        ).wait_recv()
        number = slots_in[s][:, 0:tok_dev] if tok_dev <= LANES else pltpu.repeat(slots_in[s], tok_dev // LANES, 1)
        asked += [one_where(iota((lines, tok_dev), 1) == number)] * (block // lines)
    asked = jnp.concatenate(asked, axis=0)
    line = lax.rem(lax.broadcasted_iota(jnp.int32, asked.shape, 0), block)
    picks = [
        jnp.where((line >= q * capacity) & (line < (q + 1) * capacity), asked, 0.0).astype(jnp.bfloat16)
        for q in range(n_fsdp)
    ]
    row_copies = []
    for k in range(PIECES):
        picked = jnp.zeros((n_fsdp * block, piece), F32)
        for q in range(n_fsdp):
            at = q * share + k * piece
            picked += jnp.dot(picks[q], cot[:, at : at + piece], preferred_element_type=F32)
        rows_out[:, :, k * piece : (k + 1) * piece] = picked.astype(jnp.bfloat16).reshape(n_fsdp, block, piece)
        for s in range(n_fsdp):
            copy = pltpu.make_async_remote_copy(
                rows_out.at[s, :, k * piece : (k + 1) * piece],
                rows_in.at[f, :, k * piece : (k + 1) * piece],
                rows_send.at[k, s], rows_recv.at[k, f],
                device_id=(behind, s), device_id_type=MESH,
            )
            copy.start()
            row_copies.append(copy)

    load_text.wait()

    def squares(c, total):
        value = text[:, pl.ds(pl.multiple_of(c * LANES, LANES), LANES)].astype(F32)
        return total + value * value

    total = lax.fori_loop(0, width // LANES, squares, jnp.zeros((tok_dev, LANES), F32), unroll=4)
    inv = lax.rsqrt(jnp.sum(total, axis=1, keepdims=True) / width + 1e-06)
    marks = as_column(jnp.sum(jnp.where(line < capacity, asked, 0.0), axis=0, keepdims=True))
    weight = jnp.broadcast_to(inv * (1.0 - marks), (tok_dev, LANES))

    def text_terms(c, carry):
        at = pl.ds(pl.multiple_of(c * LANES, LANES), LANES)
        terms[:, at] = fold(cot[:, at].astype(F32) * text[:, at].astype(F32) * weight)
        return carry

    lax.fori_loop(0, width // LANES, text_terms, 0, unroll=2)

    for copy in gain_copies:
        copy.wait_send()
    for d in range(1, n_fsdp):
        source = lax.rem(f + n_fsdp - d, n_fsdp)
        pltpu.make_async_remote_copy(
            gains.at[f], gains.at[source], gain_send.at[d - 1], gain_recv.at[d - 1],
            device_id=(g, source), device_id_type=MESH,
        ).wait_recv()

    gain_rows = []
    for q in range(n_fsdp):
        tiles = gains[q].astype(F32)
        flat = jnp.concatenate([tiles[c : c + 1] for c in range(tiles.shape[0])], axis=1)
        gain_rows.append([flat[:, k * piece : (k + 1) * piece] for k in range(PIECES)])

    inner = jnp.zeros((vis_dev, LANES), F32)
    for k in range(PIECES):
        cut = slice(k * piece, (k + 1) * piece)
        for s in range(n_fsdp):
            pltpu.make_async_remote_copy(
                rows_out.at[s, :, cut], rows_in.at[s, :, cut],
                rows_send.at[k, s], rows_recv.at[k, s],
                device_id=(ahead, s), device_id_type=MESH,
            ).wait_recv()
        arrived = rows_in[:, :, cut].reshape(n_fsdp * block, piece)
        for q in range(n_fsdp):
            at = q * share + k * piece
            upper = jnp.dot(places[q], arrived, preferred_element_type=F32)
            value = vision_ref[:, at : at + piece].astype(F32)
            product = upper * value
            terms[:, at : at + piece] += fold(product * inv_vision)
            product = product * gain_rows[q][k]
            for c in range(0, piece, LANES):
                inner += product[:, c : c + LANES]
            own[:, at : at + piece] = upper

    for q in range(n_fsdp):
        first_out[q] = jnp.sum(terms[:, q * share : (q + 1) * share], axis=0, keepdims=True)
    first_copies = []
    for d in range(1, n_fsdp):
        peer = lax.rem(f + d, n_fsdp)
        copy = pltpu.make_async_remote_copy(
            first_out.at[peer], first_in.at[d - 1], first_send.at[d - 1], first_recv.at[d - 1],
            device_id=(g, peer), device_id_type=MESH,
        )
        copy.start()
        first_copies.append(copy)

    inner = jnp.sum(inner, axis=1, keepdims=True) / width
    factor = inv_vision * inv_vision * inv_vision * inner
    for q in range(n_fsdp):
        for k in range(PIECES):
            at = q * share + k * piece
            scaled = own[:, at : at + piece] * gain_rows[q][k]
            value = vision_ref[:, at : at + piece].astype(F32)
            grad_ref[:, at : at + piece] = (inv_vision * scaled - value * factor).astype(jnp.bfloat16)

    part = first_out[f]
    for d in range(1, n_fsdp):
        first_copies[d - 1].wait_recv()
        part = part + first_in[d - 1]
    second[g] = part

    def send(d, carry):
        peer = lax.rem(g + d, n_grp)
        pltpu.make_async_remote_copy(
            second.at[g], second.at[g], second_send.at[peer], second_recv.at[g],
            device_id=(peer, f), device_id_type=MESH,
        ).start()
        return carry

    def arrive(d, carry):
        peer = lax.rem(g + d, n_grp)
        copy = pltpu.make_async_remote_copy(
            second.at[peer], second.at[peer], second_send.at[peer], second_recv.at[peer],
            device_id=(peer, f), device_id_type=MESH,
        )
        copy.wait_recv()
        copy.wait_send()
        return carry

    lax.fori_loop(1, n_grp, send, 0)
    for copy in slot_copies + row_copies + first_copies:
        copy.wait_send()
    lax.fori_loop(1, n_grp, arrive, 0)
    whole = second[0]
    for at in range(1, n_grp):
        whole = whole + second[at]
    share_ref[...] = whole


def shards(n_grp, n_fsdp, text, vision, vision_token, gain, cotangent):
    hop = n_grp // 4
    tok_dev, width = text.shape
    vis_dev = vision.shape[0]
    capacity = vis_dev // 4
    share = width // n_fsdp
    block = capacity * n_fsdp
    bf16 = jnp.bfloat16
    vmem, dma = pltpu.VMEM, pltpu.SemaphoreType.DMA
    inside = pl.BlockSpec(memory_space=pltpu.VMEM)
    outside = pl.BlockSpec(memory_space=pltpu.HBM)
    hbm = functools.partial(pltpu.with_memory_space_constraint, memory_space=pltpu.HBM)
    vision_grad, gain_grad = pl.pallas_call(
        functools.partial(kernel, n_grp, n_fsdp, hop, capacity),
        out_shape=(
            jax.ShapeDtypeStruct((vis_dev, width), bf16),
            jax.ShapeDtypeStruct((1, share), F32),
        ),
        in_specs=[outside] * 5,
        out_specs=(inside, inside),
        scratch_shapes=[
            vmem((tok_dev, width), bf16),
            vmem((tok_dev, width), bf16),
            vmem((vis_dev, width), bf16),
            vmem((1, vis_dev), jnp.int32),
            vmem((n_fsdp, 2 * capacity, LANES), F32),
            vmem((n_fsdp, 2 * capacity, LANES), F32),
            vmem((n_fsdp, share // LANES, LANES), bf16),
            vmem((n_fsdp, block, share), bf16),
            vmem((n_fsdp, block, share), bf16),
            vmem((vis_dev, width), F32),
            vmem((8, width), F32),
            vmem((n_fsdp, 1, share), F32),
            vmem((n_fsdp - 1, 1, share), F32),
            vmem((n_grp, 1, share), F32),
            dma((5,)),
            dma((n_fsdp,)),
            dma((n_fsdp,)),
            dma((n_fsdp - 1,)),
            dma((n_fsdp - 1,)),
            dma((PIECES, n_fsdp)),
            dma((PIECES, n_fsdp)),
            dma((n_fsdp - 1,)),
            dma((n_fsdp - 1,)),
            dma((n_grp,)),
            dma((n_grp,)),
        ],
        compiler_params=pltpu.CompilerParams(
            collective_id=0, has_side_effects=True, vmem_limit_bytes=32 * 1024 * 1024
        ),
    )(
        hbm(vision_token.reshape(1, vis_dev)), hbm(gain.reshape(share // LANES, LANES)),
        hbm(vision), hbm(text), hbm(cotangent),
    )
    return (vision_grad, gain_grad.reshape(share))


def solution(mesh):
    return jax.shard_map(
        functools.partial(shards, mesh.shape["grp"], mesh.shape["fsdp"]),
        mesh=mesh,
        in_specs=(
            P(("grp", "fsdp"), None),
            P(("grp", "fsdp"), None),
            P(("grp", "fsdp")),
            P("fsdp"),
            P(("grp", "fsdp"), None),
        ),
        out_specs=(P(("grp", "fsdp"), None), P("fsdp")),
        check_vma=False,
    )
```

```python
import functools

import jax
import jax.numpy as jnp
from jax import lax
from jax.experimental import pallas as pl
from jax.experimental.pallas import tpu as pltpu
from jax.sharding import PartitionSpec as P

MESH = pl.DeviceIdType.MESH
F32 = jnp.float32
LANES = 128
PIECES = 1


def one_where(condition):
    return jnp.where(condition, 1.0, 0.0).astype(F32)


def iota(shape, dim):
    return lax.broadcasted_iota(jnp.int32, shape, dim).astype(F32)


def as_column(row):
    n = row.shape[1]
    diagonal = iota((n, n), 0) == iota((n, n), 1)
    return jnp.sum(jnp.where(diagonal, jnp.broadcast_to(row, (n, n)), 0.0), axis=1, keepdims=True)


def fold(value):
    total = value[0:8]
    for at in range(8, value.shape[0], 8):
        total = total + value[at : at + 8]
    return total


def kernel(
    n_grp, n_fsdp, hop, capacity,
    token_hbm, gain_hbm, vision_hbm, text_hbm, cot_hbm,
    grad_ref, share_ref,
    text, cot, vision_ref, token_ref, slots_out, slots_in, gains, rows_out, rows_in, terms, vis_out, vis_in, inv_in,
    back_out, back_in, share_terms, first_out, first_in, second,
    load_sem, slot_send, slot_recv, gain_send, gain_recv, rows_send, rows_recv,
    vis_send, vis_recv, inv_send, inv_recv, back_send, back_recv,
    first_send, first_recv, second_send, second_recv,
):
    g, f = lax.axis_index("grp"), lax.axis_index("fsdp")
    tok_dev, width = text.shape
    vis_dev = vision_ref.shape[0]
    share = width // n_fsdp
    piece = share // PIECES
    block = capacity * n_fsdp
    lines = slots_out.shape[1]
    ahead, behind = lax.rem(g + hop, n_grp), lax.rem(g + n_grp - hop, n_grp)

    load_token = pltpu.make_async_copy(token_hbm, token_ref, load_sem.at[0])
    load_gain = pltpu.make_async_copy(gain_hbm, gains.at[f], load_sem.at[1])
    load_cot = pltpu.make_async_copy(cot_hbm, cot, load_sem.at[2])
    load_vision = pltpu.make_async_copy(vision_hbm, vision_ref, load_sem.at[3])
    load_text = pltpu.make_async_copy(text_hbm, text, load_sem.at[4])
    load_token.start()

    barrier = pltpu.get_barrier_semaphore()
    for s in range(n_fsdp):
        pl.semaphore_signal(barrier, inc=1, device_id=(ahead, s), device_id_type=MESH)
        pl.semaphore_signal(barrier, inc=1, device_id=(behind, s), device_id_type=MESH)
    for d in range(1, n_fsdp):
        pl.semaphore_signal(barrier, inc=1, device_id=(g, lax.rem(f + d, n_fsdp)), device_id_type=MESH)

    def greet(d, carry):
        pl.semaphore_signal(barrier, inc=1, device_id=(lax.rem(g + d, n_grp), f), device_id_type=MESH)
        return carry

    lax.fori_loop(1, n_grp, greet, 0)
    load_gain.start()
    load_cot.start()
    load_vision.start()
    load_text.start()

    load_token.wait()
    mine = token_ref[...].astype(F32) - (ahead * (n_fsdp * tok_dev)).astype(F32)
    mine_column = as_column(mine)
    target_row, target_column = jnp.zeros_like(mine), jnp.zeros_like(mine_column)
    for t in range(1, n_fsdp):
        target_row += one_where(mine >= float(t * tok_dev))
        target_column += one_where(mine_column >= float(t * tok_dev))
    square = (vis_dev, vis_dev)
    same = target_row == target_column
    rank_column = jnp.sum(
        one_where(same & (iota(square, 1) < iota(square, 0))), axis=1, keepdims=True
    )
    rank_row = jnp.sum(
        one_where(same & (iota(square, 0) < iota(square, 1))), axis=0, keepdims=True
    )
    local = mine - target_row * float(tok_dev)
    line = lax.rem(lax.broadcasted_iota(jnp.int32, (lines, vis_dev), 0), capacity).astype(F32)
    for t in range(n_fsdp):
        chosen = (line == rank_row) & (target_row == float(t))
        number = jnp.sum(jnp.where(chosen, local + 1.0, 0.0), axis=1, keepdims=True) - 1.0
        slots_out[t] = jnp.broadcast_to(number, (lines, LANES))
    pl.semaphore_wait(barrier, 3 * n_fsdp + n_grp - 2)

    slot_copies = []
    for s in range(n_fsdp):
        copy = pltpu.make_async_remote_copy(
            slots_out.at[s], slots_in.at[f], slot_send.at[s], slot_recv.at[f],
            device_id=(ahead, s), device_id_type=MESH,
        )
        copy.start()
        slot_copies.append(copy)
    load_gain.wait()
    gain_copies = []
    for d in range(1, n_fsdp):
        copy = pltpu.make_async_remote_copy(
            gains.at[f], gains.at[f], gain_send.at[d - 1], gain_recv.at[d - 1],
            device_id=(g, lax.rem(f + d, n_fsdp)), device_id_type=MESH,
        )
        copy.start()
        gain_copies.append(copy)

    load_cot.wait()

    asked = []
    for s in range(n_fsdp):
        pltpu.make_async_remote_copy(
            slots_out.at[s], slots_in.at[s], slot_send.at[s], slot_recv.at[s],
            device_id=(behind, s), device_id_type=MESH,
        ).wait_recv()
        number = slots_in[s][:, 0:tok_dev] if tok_dev <= LANES else pltpu.repeat(slots_in[s], tok_dev // LANES, 1)
        asked.append(one_where(iota((lines, tok_dev), 1) == number)[0:capacity])
    asked = jnp.concatenate(asked, axis=0)
    picks = asked.astype(jnp.bfloat16)
    row_copies = []
    for k in range(PIECES):
        cut = slice(k * piece, (k + 1) * piece)
        for s in range(n_fsdp):
            at = s * share + k * piece
            picked = jnp.dot(picks, cot[:, at : at + piece], preferred_element_type=F32)
            rows_out[s, :, cut] = picked.astype(jnp.bfloat16)
        for s in range(n_fsdp):
            copy = pltpu.make_async_remote_copy(
                rows_out.at[s, :, cut], rows_in.at[f, :, cut], rows_send.at[k, s], rows_recv.at[k, f],
                device_id=(behind, s), device_id_type=MESH,
            )
            copy.start()
            row_copies.append(copy)

    load_vision.wait()
    slot_row = target_row * float(capacity) + rank_row
    slot_column = target_column * float(capacity) + rank_column
    gather = one_where(iota((block, vis_dev), 0) == slot_row).astype(jnp.bfloat16)
    scatter = one_where(iota((vis_dev, block), 1) == slot_column).astype(jnp.bfloat16)
    total = jnp.zeros((block, LANES), F32)
    for q in range(n_fsdp):
        for k in range(PIECES):
            at = q * share + k * piece
            value = jnp.dot(gather, vision_ref[:, at : at + piece], preferred_element_type=F32)
            vis_out[q, :, k * piece : (k + 1) * piece] = value.astype(jnp.bfloat16)
            for c in range(0, piece, LANES):
                total += value[:, c : c + LANES] * value[:, c : c + LANES]
    inv_vision = lax.rsqrt(jnp.sum(total, axis=1, keepdims=True) / width + 1e-06)
    inv_in[f] = jnp.broadcast_to(inv_vision, (block, LANES))
    vis_in[f] = vis_out[f]
    vis_copies = []
    for d in range(1, n_fsdp):
        peer = lax.rem(f + d, n_fsdp)
        for source, target, send_sem, recv_sem in (
            (vis_out.at[peer], vis_in.at[f], vis_send, vis_recv),
            (inv_in.at[f], inv_in.at[f], inv_send, inv_recv),
        ):
            copy = pltpu.make_async_remote_copy(
                source, target, send_sem.at[d - 1], recv_sem.at[d - 1],
                device_id=(g, peer), device_id_type=MESH,
            )
            copy.start()
            vis_copies.append(copy)

    load_text.wait()

    def squares(c, total):
        value = text[:, pl.ds(pl.multiple_of(c * LANES, LANES), LANES)].astype(F32)
        return total + value * value

    total = lax.fori_loop(0, width // LANES, squares, jnp.zeros((tok_dev, LANES), F32), unroll=4)
    inv = lax.rsqrt(jnp.sum(total, axis=1, keepdims=True) / width + 1e-06)
    marks = as_column(jnp.sum(asked, axis=0, keepdims=True))
    weight = jnp.broadcast_to(inv * (1.0 - marks), (tok_dev, LANES))

    def text_terms(c, carry):
        at = pl.ds(pl.multiple_of(c * LANES, LANES), LANES)
        terms[:, at] = fold(cot[:, at].astype(F32) * text[:, at].astype(F32) * weight)
        return carry

    lax.fori_loop(0, width // LANES, text_terms, 0, unroll=2)

    for q in range(n_fsdp):
        first_out[q] = jnp.sum(terms[:, q * share : (q + 1) * share], axis=0, keepdims=True)
    first_copies = []
    for d in range(1, n_fsdp):
        peer = lax.rem(f + d, n_fsdp)
        copy = pltpu.make_async_remote_copy(
            first_out.at[peer], first_in.at[d - 1], first_send.at[d - 1], first_recv.at[d - 1],
            device_id=(g, peer), device_id_type=MESH,
        )
        copy.start()
        first_copies.append(copy)

    for copy in gain_copies:
        copy.wait_send()
    for d in range(1, n_fsdp):
        source = lax.rem(f + n_fsdp - d, n_fsdp)
        pltpu.make_async_remote_copy(
            gains.at[f], gains.at[source], gain_send.at[d - 1], gain_recv.at[d - 1],
            device_id=(g, source), device_id_type=MESH,
        ).wait_recv()

    gain_rows = []
    for q in range(n_fsdp):
        tiles = gains[q].astype(F32)
        flat = jnp.concatenate([tiles[c : c + 1] for c in range(tiles.shape[0])], axis=1)
        gain_rows.append([flat[:, k * piece : (k + 1) * piece] for k in range(PIECES)])

    for d in range(1, n_fsdp):
        source = lax.rem(f + n_fsdp - d, n_fsdp)
        pltpu.make_async_remote_copy(
            vis_in.at[source], vis_in.at[source], vis_send.at[d - 1], vis_recv.at[d - 1],
            device_id=(g, source), device_id_type=MESH,
        ).wait_recv()
        pltpu.make_async_remote_copy(
            inv_in.at[source], inv_in.at[source], inv_send.at[d - 1], inv_recv.at[d - 1],
            device_id=(g, source), device_id_type=MESH,
        ).wait_recv()
    part = first_out[f]
    for d in range(1, n_fsdp):
        first_copies[d - 1].wait_recv()
        part = part + first_in[d - 1]

    every = n_fsdp * block
    to = lax.broadcasted_iota(jnp.int32, (every, every), 0)
    within = lax.rem(to, block)
    place = lax.rem(within, capacity)
    origin = (within - place) * n_fsdp + lax.div(to - within, n_fsdp) + place
    order = one_where(lax.broadcasted_iota(jnp.int32, (every, every), 1) == origin).astype(jnp.bfloat16)
    inv_all = inv_in[...].reshape(every, LANES)[:, 0:1]
    back_copies = []
    for k in range(PIECES):
        cut = slice(k * piece, (k + 1) * piece)
        for s in range(n_fsdp):
            pltpu.make_async_remote_copy(
                rows_out.at[s, :, cut], rows_in.at[s, :, cut], rows_send.at[k, s], rows_recv.at[k, s],
                device_id=(ahead, s), device_id_type=MESH,
            ).wait_recv()
        upper = jnp.dot(order, rows_in[:, :, cut].reshape(every, piece), preferred_element_type=F32)
        back_out[:, :, cut] = upper.astype(jnp.bfloat16).reshape(n_fsdp, block, piece)
        for d in range(1, n_fsdp):
            peer = lax.rem(f + d, n_fsdp)
            copy = pltpu.make_async_remote_copy(
                back_out.at[peer, :, cut], back_in.at[f, :, cut],
                back_send.at[k, d - 1], back_recv.at[k, d - 1],
                device_id=(g, peer), device_id_type=MESH,
            )
            copy.start()
            back_copies.append(copy)
        value = vis_in[:, :, cut].reshape(every, piece).astype(F32)
        share_terms[:, cut] = jnp.sum(upper * value * inv_all, axis=0, keepdims=True)
    second[g] = part + share_terms[...]

    def send(d, carry):
        peer = lax.rem(g + d, n_grp)
        pltpu.make_async_remote_copy(
            second.at[g], second.at[g], second_send.at[peer], second_recv.at[g],
            device_id=(peer, f), device_id_type=MESH,
        ).start()
        return carry

    def arrive(d, carry):
        peer = lax.rem(g + d, n_grp)
        copy = pltpu.make_async_remote_copy(
            second.at[peer], second.at[peer], second_send.at[peer], second_recv.at[peer],
            device_id=(peer, f), device_id_type=MESH,
        )
        copy.wait_recv()
        copy.wait_send()
        return carry

    lax.fori_loop(1, n_grp, send, 0)
    back_in[f] = back_out[f]
    for k in range(PIECES):
        for d in range(1, n_fsdp):
            source = lax.rem(f + n_fsdp - d, n_fsdp)
            cut = slice(k * piece, (k + 1) * piece)
            pltpu.make_async_remote_copy(
                back_in.at[source, :, cut], back_in.at[source, :, cut],
                back_send.at[k, d - 1], back_recv.at[k, d - 1],
                device_id=(g, source), device_id_type=MESH,
            ).wait_recv()
    inner = jnp.zeros((block, LANES), F32)
    for q in range(n_fsdp):
        for k in range(PIECES):
            cut = slice(k * piece, (k + 1) * piece)
            product = back_in[q, :, cut].astype(F32) * vis_out[q, :, cut].astype(F32) * gain_rows[q][k]
            for c in range(0, piece, LANES):
                inner += product[:, c : c + LANES]
    inner = jnp.sum(inner, axis=1, keepdims=True) / width
    factor = inv_vision * inv_vision * inv_vision * inner
    for q in range(n_fsdp):
        for k in range(PIECES):
            cut = slice(k * piece, (k + 1) * piece)
            scaled = back_in[q, :, cut].astype(F32) * gain_rows[q][k]
            grad = (inv_vision * scaled - vis_out[q, :, cut].astype(F32) * factor).astype(jnp.bfloat16)
            at = q * share + k * piece
            grad_ref[:, at : at + piece] = jnp.dot(scatter, grad, preferred_element_type=F32).astype(jnp.bfloat16)
    for copy in slot_copies + row_copies + first_copies + vis_copies + back_copies:
        copy.wait_send()
    lax.fori_loop(1, n_grp, arrive, 0)
    whole = second[0]
    for at in range(1, n_grp):
        whole = whole + second[at]
    share_ref[...] = whole


def shards(n_grp, n_fsdp, text, vision, vision_token, gain, cotangent):
    hop = n_grp // 4
    tok_dev, width = text.shape
    vis_dev = vision.shape[0]
    capacity = vis_dev // 4
    share = width // n_fsdp
    block = capacity * n_fsdp
    bf16 = jnp.bfloat16
    vmem, dma = pltpu.VMEM, pltpu.SemaphoreType.DMA
    inside = pl.BlockSpec(memory_space=pltpu.VMEM)
    outside = pl.BlockSpec(memory_space=pltpu.HBM)
    hbm = functools.partial(pltpu.with_memory_space_constraint, memory_space=pltpu.HBM)
    vision_grad, gain_grad = pl.pallas_call(
        functools.partial(kernel, n_grp, n_fsdp, hop, capacity),
        out_shape=(
            jax.ShapeDtypeStruct((vis_dev, width), bf16),
            jax.ShapeDtypeStruct((1, share), F32),
        ),
        in_specs=[outside] * 5,
        out_specs=(inside, inside),
        scratch_shapes=[
            vmem((tok_dev, width), bf16),
            vmem((tok_dev, width), bf16),
            vmem((vis_dev, width), bf16),
            vmem((1, vis_dev), jnp.int32),
            vmem((n_fsdp, 2 * capacity, LANES), F32),
            vmem((n_fsdp, 2 * capacity, LANES), F32),
            vmem((n_fsdp, share // LANES, LANES), bf16),
            vmem((n_fsdp, block, share), bf16),
            vmem((n_fsdp, block, share), bf16),
            vmem((8, width), F32),
            vmem((n_fsdp, block, share), bf16),
            vmem((n_fsdp, block, share), bf16),
            vmem((n_fsdp, block, LANES), F32),
            vmem((n_fsdp, block, share), bf16),
            vmem((n_fsdp, block, share), bf16),
            vmem((1, share), F32),
            vmem((n_fsdp, 1, share), F32),
            vmem((n_fsdp - 1, 1, share), F32),
            vmem((n_grp, 1, share), F32),
            dma((5,)),
            dma((n_fsdp,)),
            dma((n_fsdp,)),
            dma((n_fsdp - 1,)),
            dma((n_fsdp - 1,)),
            dma((PIECES, n_fsdp)),
            dma((PIECES, n_fsdp)),
            dma((n_fsdp - 1,)),
            dma((n_fsdp - 1,)),
            dma((n_fsdp - 1,)),
            dma((n_fsdp - 1,)),
            dma((PIECES, n_fsdp - 1)),
            dma((PIECES, n_fsdp - 1)),
            dma((n_fsdp - 1,)),
            dma((n_fsdp - 1,)),
            dma((n_grp,)),
            dma((n_grp,)),
        ],
        compiler_params=pltpu.CompilerParams(
            collective_id=0, has_side_effects=True, vmem_limit_bytes=32 * 1024 * 1024
        ),
    )(
        hbm(vision_token.reshape(1, vis_dev)), hbm(gain.reshape(share // LANES, LANES)),
        hbm(vision), hbm(text), hbm(cotangent),
    )
    return (vision_grad, gain_grad.reshape(share))


def solution(mesh):
    return jax.shard_map(
        functools.partial(shards, mesh.shape["grp"], mesh.shape["fsdp"]),
        mesh=mesh,
        in_specs=(
            P(("grp", "fsdp"), None),
            P(("grp", "fsdp"), None),
            P(("grp", "fsdp")),
            P("fsdp"),
            P(("grp", "fsdp"), None),
        ),
        out_specs=(P(("grp", "fsdp"), None), P("fsdp")),
        check_vma=False,
    )
```
